256 devices in a mesh: grp: 16 (over y_lo, x, core), tok: 16 (over z, y_hi).
Axes of the slice: x: 4, y: 4 (y_hi: 2, y_lo: 2; y = y_hi * 2 + y_lo), z: 8, core: 2. Of those that a mesh axis runs over, the one named last changes fastest.
Arguments:
- acts: bfloat16 [4096, 8192], P('tok', 'grp'), may hold values from -6 to 6
- grads: bfloat16 [4096, 8192], P('tok', 'grp'), may hold values from -6 to 6
- basis_in: bfloat16 [8192, 8192], P('tok', 'grp'), may hold values from -0.0625 to 0.0625
- basis_out: bfloat16 [8192, 8192], P('tok', 'grp'), may hold values from -0.0625 to 0.0625
- membership: int32 [16, 256], P('tok'), may hold values from 0 to 1, as said below
Outputs:
- eigen_values: float32 [8192, 16, 512], P('grp', None, 'tok')
The draws below stay inside these ranges and needn't reach their ends.
Inputs may be any that keep to these rules, and one draw needn't show every extreme that they name: `membership`: along each row u the numbers never fall and both 0 and 1 appear; each sequence holds 64 to 192 rows, and in every draw some sequence holds exactly 192.
All inputs are finite; a program needn't handle non-finite values.
Results may differ from the reference program's by a relative error of at most 0.0017.
Values may be sent and summed in bfloat16 or wider, within the bound.
A program may use at most 128 MiB of HBM per device.

```python
import jax
import jax.numpy as jnp
from jax import lax

D = 8192
ROWS = 256
SEQ_DEV = 2
SHARDS = 16
GROUPS = 16
PANEL = 512
TOKENS = 4096


def draw_membership(key, part):
    key = jax.random.fold_in(key, 7)
    key_len, key_pick, key_side = jax.random.split(key, 3)
    lowest = ROWS // 4
    highest = 3 * ROWS // 4
    lengths = jax.random.randint(key_len, (SHARDS,), lowest, highest + 1)
    picked = jax.random.randint(key_pick, (), 0, SHARDS)
    side_bit = jax.random.randint(key_side, (), 0, 2)
    forced = jnp.where(side_bit == 0, highest, ROWS - highest)
    lengths = jnp.where(jnp.arange(SHARDS) == picked, forced, lengths)
    positions = jnp.arange(ROWS)[None, :]
    return (positions >= lengths[:, None]).astype(jnp.int32)


def level_of(own_key, dims, cuts, smallest, high):
    level, own = 1.0, jax.random.fold_in(own_key, 6)
    for axis_at, blocks in cuts:
        draws = jnp.exp(jax.random.uniform(jax.random.fold_in(own, axis_at), (blocks,), jnp.float32, smallest / len(cuts), high / len(cuts)))
        level = level * jnp.repeat(draws, dims[axis_at] // blocks).reshape([-1 if axis == axis_at else 1 for axis in range(len(dims))])
    return level


def normal_values(rng, dims, scale, reach, cuts=(), dtype=jnp.bfloat16):
    result = scale * jax.random.normal(rng, dims, jnp.float32)
    if cuts:
        result = result * level_of(rng, dims, cuts, -0.22, 0.18)
    return jnp.clip(result, -reach, reach).astype(dtype)


def setup_inputs(seed: int = 0) -> dict:
    key_of = jax.random.split(jax.random.key(seed), 6)
    return {
        "acts": normal_values(key_of[0], (TOKENS, D), 1.0, 6.0, ((0, 16), (1, 16))),
        "grads": normal_values(key_of[1], (TOKENS, D), 1.0, 6.0, ((0, 16), (1, 16))),
        "basis_in": normal_values(key_of[2], (D, D), D ** -0.5, 0.0625, ((0, 16), (1, 16))),
        "basis_out": normal_values(key_of[3], (D, D), D ** -0.5, 0.0625, ((0, 16), (1, 16))),
        "membership": draw_membership(jax.random.fold_in(key_of[5], 71), 0),
    }


def reference(acts, grads, basis_in, basis_out, membership):
    rotated_in = jnp.dot(acts, basis_in, preferred_element_type=jnp.float32).astype(jnp.bfloat16)
    rotated_out = jnp.dot(grads, basis_out, preferred_element_type=jnp.float32).astype(jnp.bfloat16)
    shards = membership.shape[0]
    rows = membership.shape[1]
    blocks_in = rotated_in.reshape(shards, rows, D)
    blocks_out = rotated_out.reshape(shards, rows, D)

    def one_block(total, items):
        block_in, block_out, labels = items
        for seq_index in range(SEQ_DEV):
            keep = (labels == seq_index)[:, None]
            masked = jnp.where(keep, block_in, jnp.zeros_like(block_in))
            moment = jnp.dot(block_out.T, masked, preferred_element_type=jnp.float32)
            total = total + moment * moment
        return total, None

    start = jnp.zeros((D, D), jnp.float32)
    total, _ = lax.scan(one_block, start, (blocks_in, blocks_out, membership))
    total = total / jnp.float32(TOKENS)
    return total.reshape(D, GROUPS, PANEL)
```

```python
import jax
import jax.numpy as jnp
from jax import lax
from jax.experimental import pallas as pl
from jax.experimental.pallas import tpu as pltpu
from jax.sharding import PartitionSpec as P

MESH = pl.DeviceIdType.MESH
F32, BF16 = jnp.float32, jnp.bfloat16
NSEM = 160


def kernel(acts, grads, basis_in, basis_out, own_labels, out, a_buf, b_buf, part, landed, rot_out,
           rin_send, rot_in, labels, ssem, rsem, lsem):
    g, t = lax.axis_index("grp"), lax.axis_index("tok")
    c, x, yl = lax.rem(g, 2), lax.rem(lax.div(g, 2), 4), lax.div(g, 8)
    z, yh = lax.div(t, 2), lax.rem(t, 2)

    def grp(x_, yl_, c_):
        return (yl_ * 4 + x_) * 2 + c_

    def xat(step):
        return lax.rem(x + 4 + step, 4)

    def zat(step):
        return lax.rem(z + 8 + step, 8)

    to_x = {1: {"grp": grp(xat(1), yl, c)}, -1: {"grp": grp(xat(-1), yl, c)}}
    to_z = {1: {"tok": zat(1) * 2 + yh}, -1: {"tok": zat(-1) * 2 + yh}}
    to_yl = {"grp": grp(x, 1 - yl, c)}
    to_yh = {"tok": z * 2 + 1 - yh}
    to_sib = {"grp": grp(x, yl, 1 - c)}
    to_diag = {"grp": grp(x, yl, 1 - c), "tok": z * 2 + 1 - yh}
    to_tok = [None] + [{"tok": lax.rem(t + d, 16)} for d in range(1, 16)]

    barrier = pltpu.get_barrier_semaphore()
    partners = to_tok[1:] + [to_diag, to_x[1], to_x[-1], to_yl, to_sib]
    for partner in partners:
        pl.semaphore_signal(barrier, inc=1, device_id=partner, device_id_type=MESH)
    pl.semaphore_wait(barrier, len(partners))

    used = [0]
    sent = []

    def make(src, dst, dev):
        at = used[0]
        used[0] += 1
        return pltpu.make_async_remote_copy(
            src_ref=src, dst_ref=dst, send_sem=ssem.at[at], recv_sem=rsem.at[at],
            device_id=dev, device_id_type=MESH)

    def send(src, dst, dev):
        copy = make(src, dst, dev)
        copy.start()
        sent.append(copy)
        return copy

    feats, bases = (acts, grads), (basis_in, basis_out)

    ring = {}

    def half_of(d, first):
        return 0 if (d == 1) == first else 1

    def b_send(m, s, first):
        for d in (1, -1):
            if s == 4 and not first:
                continue
            rows = pl.ds(half_of(d, first) * 256, 256)
            block = zat(-(s - 1) * d)
            src = bases[m].at[rows] if s == 1 else b_buf.at[m, block, rows]
            ring[m, s, first, d] = send(src, b_buf.at[m, block, rows], to_z[d])

    def b_wait(m, s, first):
        for d in (1, -1):
            ring[m, s, first, d].wait_recv()

    def b_pass(m, s, first):
        b_wait(m, s, first)
        b_send(m, s + 1, first)

    b_send(0, 1, True)
    b_send(0, 1, False)

    diag = [make(feats[m], a_buf.at[m, yh, x, yl], to_diag) for m in range(2)]
    stay = [pltpu.make_async_copy(feats[m], a_buf.at[m, yh, x, yl], lsem.at[m]) for m in range(2)]
    keep = [pltpu.make_async_copy(bases[m], b_buf.at[m, z], lsem.at[2 + m]) for m in range(2)]

    @pl.when(yh != c)
    def _():
        for m in range(2):
            diag[m].start()

    @pl.when(yh == c)
    def _():
        for m in range(2):
            stay[m].start()

    for copy in keep:
        copy.start()
    label_copies = [None]
    for d in range(1, 16):
        label_copies.append(send(own_labels, labels.at[t], to_tok[d]))
    labels[t] = own_labels[...]
    part[...] = jnp.zeros_like(part)
    out[...] = jnp.zeros_like(out)

    feat = {}

    def a_diag_wait(m):
        @pl.when(yh != c)
        def _():
            diag[m].wait()

        @pl.when(yh == c)
        def _():
            stay[m].wait()

    def a_yl(m):
        mine = a_buf.at[m, c, x, yl]
        feat[m, "yl"] = send(mine, mine, to_yl)

    def a_x1(m):
        feat[m, "yl"].wait_recv()
        mine = a_buf.at[m, c, x]
        for d in (1, -1):
            feat[m, "x1", d] = send(mine, mine, to_x[d])

    def a_x2(m):
        for d in (1, -1):
            feat[m, "x1", d].wait_recv()
        for d, lane in ((1, 0), (-1, 1)):
            moved = a_buf.at[m, c, xat(-d), lane]
            feat[m, "x2", d] = send(moved, moved, to_x[d])

    def a_sib(m):
        for d in (1, -1):
            feat[m, "x2", d].wait_recv()
        mine = a_buf.at[m, c]
        feat[m, "sib"] = send(mine, mine, to_sib)

    def multiply(m, block):
        xb, yb = lax.rem(block, 4), lax.div(block, 4)
        for half in range(2):
            part[m, half] += jnp.dot(a_buf[m, half, xb, yb], b_buf[m, block], preferred_element_type=F32)

    def multiply_near(m, lo, hi):
        @pl.loop(lo, hi)
        def _(step):
            multiply(m, lax.rem(z + 8 + step, 8))

    def multiply_pair(m, step):
        @pl.loop(0, 2)
        def _(way):
            multiply(m, lax.rem(z + 8 + step * (1 - 2 * way), 8))

    reduce = {}

    def r_send(m, nh):
        cols = pl.ds(nh * 256, 256)
        reduce[m, nh] = send(part.at[m, 1 - yh, :, cols], landed.at[m, :, cols], to_yh)

    def rotated(m, nh):
        reduce[m, nh].wait_recv()
        cols = pl.ds(nh * 256, 256)
        total = part[m, yh, :, cols] + landed[m, :, cols]
        return jnp.transpose(total).astype(BF16)

    rin = {}

    def i_slices():
        for nh in range(2):
            rin_send[pl.ds(nh * 8, 8)] = rotated(0, nh).reshape(8, 32, 256)
        for d in range(1, 16):
            rin[d] = send(rin_send.at[lax.rem(t + d, 16)], rot_in.at[x, yl, c, t], to_tok[d])
        rot_in[x, yl, c, t] = rin_send[t]

    def i_yl():
        for d in range(1, 16):
            rin[d].wait_recv()
        mine = rot_in.at[x, yl, c]
        rin["yl"] = send(mine, mine, to_yl)

    def i_x1():
        rin["yl"].wait_recv()
        mine = rot_in.at[x, :, c]
        for d in (1, -1):
            rin["x1", d] = send(mine, mine, to_x[d])

    def i_x2():
        for d in (1, -1):
            rin["x1", d].wait_recv()
        for d, lane in ((1, 0), (-1, 1)):
            moved = rot_in.at[xat(-d), lane, c]
            rin["x2", d] = send(moved, moved, to_x[d])

    def i_sib():
        for d in (1, -1):
            rin["x2", d].wait_recv()
        mine = rot_in.at[:, :, c]
        rin["sib"] = send(mine, mine, to_sib)

    a_diag_wait(0)
    a_yl(0)
    b_pass(0, 1, True)
    a_diag_wait(1)
    a_yl(1)
    a_x1(0)
    b_pass(0, 1, False)
    b_pass(0, 2, True)
    a_x2(0)
    b_pass(0, 2, False)
    a_sib(0)
    a_x1(1)
    b_pass(0, 3, True)
    for copy in keep:
        copy.wait()
    feat[0, "sib"].wait_recv()
    multiply_near(0, -2, 3)
    b_wait(0, 3, False)
    b_send(1, 1, True)
    b_send(1, 1, False)
    multiply_pair(0, 3)
    b_wait(0, 4, True)
    multiply(0, zat(4))
    r_send(0, 0)
    r_send(0, 1)
    a_x2(1)
    b_pass(1, 1, True)
    a_sib(1)
    b_pass(1, 1, False)
    i_slices()
    feat[1, "sib"].wait_recv()
    multiply_near(1, -1, 2)
    b_pass(1, 2, True)
    i_yl()
    b_pass(1, 2, False)
    multiply_pair(1, 2)
    i_x1()
    b_pass(1, 3, True)
    i_x2()
    b_wait(1, 3, False)
    multiply_pair(1, 3)
    b_wait(1, 4, True)
    multiply(1, zat(4))
    r_send(1, 1)
    r_send(1, 0)
    i_sib()

    low, high = pl.ds(0, 256), pl.ds(256, 256)
    gat = {}

    def o_single(s):
        for d in (1, -1):
            block = 2 * zat(-(s - 1) * d) + yh
            rows = high if s < 4 else pl.ds(256 if d == 1 else 384, 128)
            ref = rot_out.at[block, rows]
            gat["s", s, d] = send(ref, ref, to_z[d])

    def o_cross(s):
        for d in ((1, -1) if s in (1, 2, 3) else (1,)):
            ref = rot_out.at[2 * zat(-s * d) + yh, high]
            gat["c", s, d] = send(ref, ref, to_yh)

    def o_pair(s):
        for d in (1, -1):
            block = zat(-(s - 1) * d)
            ref = rot_out.at[pl.ds(2 * block, 2), low] if s < 4 else rot_out.at[2 * block + (d < 0), low]
            gat["p", s, d] = send(ref, ref, to_z[d])

    def o_wait(kind, s):
        for d in (1, -1):
            if (kind, s, d) in gat:
                gat[kind, s, d].wait_recv()

    rot_out[t, high] = rotated(1, 1)
    o_single(1)
    o_cross(0)
    rot_out[t, low] = rotated(1, 0)
    ref = rot_out.at[t, low]
    lower = send(ref, ref, to_yh)
    o_wait("s", 1)
    o_single(2)
    o_cross(1)
    lower.wait_recv()
    o_pair(1)
    o_wait("s", 2)
    o_single(3)
    o_cross(2)
    o_wait("p", 1)
    o_pair(2)
    o_wait("s", 3)
    o_single(4)
    o_cross(3)
    o_wait("p", 2)
    o_pair(3)

    def moments(u):
        mine = rot_in[:, :, :, u].reshape(512, 256)
        second = labels[u][0:1].astype(BF16)
        for keep_mask in (second, 1.0 - second):
            masked = mine * keep_mask
            for half in range(2):
                rows = pl.ds(half * 256, 256)
                moment = lax.dot_general(rot_out[u, rows], masked, (((1,), (1,)), ((), ())),
                                         preferred_element_type=F32)
                out[rows] += moment * moment

    def moments_at(step):
        @pl.loop(0, 2)
        def _(j):
            moments(2 * lax.rem(z + 8 + step, 8) + j)

    for d in range(1, 16):
        label_copies[d].wait_recv()
    rin["sib"].wait_recv()
    o_wait("c", 0)
    moments_at(0)
    o_wait("s", 4)
    o_cross(4)
    o_wait("p", 3)
    o_pair(4)
    for s in (1, 2, 3):
        o_wait("c", s)
        moments_at(s)
        moments_at(-s)
    o_wait("p", 4)
    o_wait("c", 4)
    moments_at(4)
    out[...] = out[...] * F32(1.0 / 4096)
    for copy in sent:
        copy.wait_send()


def local(acts, grads, basis_in, basis_out, membership):
    own_labels = jnp.broadcast_to(membership, (8, 256)).astype(F32)
    any_space, vmem = pl.BlockSpec(memory_space=pl.ANY), pl.BlockSpec(memory_space=pltpu.VMEM)
    energy = pl.pallas_call(
        kernel,
        out_shape=jax.ShapeDtypeStruct((512, 512), F32),
        in_specs=[any_space] * 4 + [vmem],
        out_specs=vmem,
        scratch_shapes=[
            pltpu.VMEM((2, 2, 4, 2, 256, 512), BF16),
            pltpu.VMEM((2, 8, 512, 512), BF16),
            pltpu.VMEM((2, 2, 256, 512), F32),
            pltpu.VMEM((2, 256, 512), F32),
            pltpu.VMEM((16, 512, 256), BF16),
            pltpu.VMEM((16, 32, 256), BF16),
            pltpu.VMEM((4, 2, 2, 16, 32, 256), BF16),
            pltpu.VMEM((16, 8, 256), F32),
            pltpu.SemaphoreType.DMA((NSEM,)),
            pltpu.SemaphoreType.DMA((NSEM,)),
            pltpu.SemaphoreType.DMA((4,)),
        ],
        compiler_params=pltpu.CompilerParams(
            collective_id=0, has_side_effects=True, vmem_limit_bytes=56 * 1024 * 1024),
        name="ekfac",
    )(acts, grads, basis_in, basis_out, own_labels)
    return energy.reshape(512, 4, 2, 2, 32).transpose(0, 2, 1, 3, 4).reshape(512, 16, 32)


def solution(mesh):
    placed = (P("tok", "grp"), P("tok", "grp"), P("tok", "grp"), P("tok", "grp"), P("tok", None))
    return jax.shard_map(
        local, mesh=mesh, in_specs=placed, out_specs=P("grp", None, "tok"), check_vma=False
    )
```

```python
import jax
import jax.numpy as jnp
from jax import lax
from jax.experimental import pallas as pl
from jax.experimental.pallas import tpu as pltpu
from jax.sharding import PartitionSpec as P

MESH = pl.DeviceIdType.MESH
F32, BF16 = jnp.float32, jnp.bfloat16
NSEM = 200


def kernel(acts, grads, basis_in, basis_out, membership, out, a_buf, b_buf, part, landed, rot_out,
           rin_send, rot_in, labels, ssem, rsem, lsem):
    g, t = lax.axis_index("grp"), lax.axis_index("tok")
    c, x, yl = lax.rem(g, 2), lax.rem(lax.div(g, 2), 4), lax.div(g, 8)
    z, yh = lax.div(t, 2), lax.rem(t, 2)

    def grp(x_, yl_, c_):
        return (yl_ * 4 + x_) * 2 + c_

    def xat(step):
        return lax.rem(x + 4 + step, 4)

    def zat(step):
        return lax.rem(z + 8 + step, 8)

    to_x = {1: {"grp": grp(xat(1), yl, c)}, -1: {"grp": grp(xat(-1), yl, c)}}
    to_z = {1: {"tok": zat(1) * 2 + yh}, -1: {"tok": zat(-1) * 2 + yh}}
    to_yl = {"grp": grp(x, 1 - yl, c)}
    to_yh = {"tok": z * 2 + 1 - yh}
    to_sib = {"grp": grp(x, yl, 1 - c)}
    to_diag = {"grp": grp(x, yl, 1 - c), "tok": z * 2 + 1 - yh}
    to_tok = [None] + [{"tok": lax.rem(t + d, 16)} for d in range(1, 16)]

    barrier = pltpu.get_barrier_semaphore()
    partners = to_tok[1:] + [to_diag, to_x[1], to_x[-1], to_yl, to_sib]
    for partner in partners:
        pl.semaphore_signal(barrier, inc=1, device_id=partner, device_id_type=MESH)
    pl.semaphore_wait(barrier, len(partners))

    used = [0]
    sent = []

    def make(src, dst, dev):
        at = used[0]
        used[0] += 1
        return pltpu.make_async_remote_copy(
            src_ref=src, dst_ref=dst, send_sem=ssem.at[at], recv_sem=rsem.at[at],
            device_id=dev, device_id_type=MESH)

    def send(src, dst, dev):
        copy = make(src, dst, dev)
        copy.start()
        sent.append(copy)
        return copy

    feats, bases = (acts, grads), (basis_in, basis_out)

    ring = {}

    def b_part(k, block, first, d):
        half = 0 if (d == 1) == first else 1
        if k == 0:
            cols = pl.ds(half * 256, 256)
            return basis_in.at[:, cols], b_buf.at[0, half, block]
        rows, cols = pl.ds(half * 256, 256), pl.ds((k - 1) * 256, 256)
        return basis_out.at[rows, cols], b_buf.at[1, k - 1, block, rows]

    def b_send(k, s, first):
        for d in (1, -1):
            if s == 4 and not first:
                continue
            source, slot = b_part(k, zat(-(s - 1) * d), first, d)
            ring[k, s, first, d] = send(source if s == 1 else slot, slot, to_z[d])

    def b_wait(k, s, first):
        for d in (1, -1):
            ring[k, s, first, d].wait_recv()

    def b_pass(k, s, first):
        b_wait(k, s, first)
        b_send(k, s + 1, first)

    b_send(0, 1, True)
    b_send(0, 1, False)

    diag = [make(feats[m], a_buf.at[m, yh, x, yl], to_diag) for m in range(2)]
    stay = [pltpu.make_async_copy(feats[m], a_buf.at[m, yh, x, yl], lsem.at[m]) for m in range(2)]
    keep = [pltpu.make_async_copy(bases[m].at[:, pl.ds(nh * 256, 256)], b_buf.at[m, nh, z], lsem.at[2 + 2 * m + nh])
            for m in range(2) for nh in range(2)]

    @pl.when(yh != c)
    def _():
        for m in range(2):
            diag[m].start()

    @pl.when(yh == c)
    def _():
        for m in range(2):
            stay[m].start()

    for copy in keep:
        copy.start()
    labels[t] = membership[...]
    mine = labels.at[t]
    label_copies = [None] + [send(mine, mine, to_tok[d]) for d in range(1, 16)]
    part[...] = jnp.zeros_like(part)
    out[...] = jnp.zeros_like(out)

    feat = {}

    def a_diag_wait(m):
        @pl.when(yh != c)
        def _():
            diag[m].wait()

        @pl.when(yh == c)
        def _():
            stay[m].wait()

    def a_own(m):
        a_diag_wait(m)
        mine = a_buf.at[m, c, x, yl]
        feat[m, "yl"] = send(mine, mine, to_yl)
        for d in (1, -1):
            feat[m, "own", d] = send(mine, mine, to_x[d])

    def a_other(m):
        feat[m, "yl"].wait_recv()
        theirs = a_buf.at[m, c, x, 1 - yl]
        for d in (1, -1):
            feat[m, "other", d] = send(theirs, theirs, to_x[d])

    def a_x2(m):
        for d in (1, -1):
            feat[m, "own", d].wait_recv()
            feat[m, "other", d].wait_recv()
        for d, lane in ((1, 0), (-1, 1)):
            moved = a_buf.at[m, c, xat(-d), lane]
            feat[m, "x2", d] = send(moved, moved, to_x[d])

    def a_sib(m):
        for d in (1, -1):
            feat[m, "x2", d].wait_recv()
        mine = a_buf.at[m, c]
        feat[m, "sib"] = send(mine, mine, to_sib)

    def multiply(m, halves, block):
        xb, yb = lax.rem(block, 4), lax.div(block, 4)
        for nh in halves:
            for half in range(2):
                part[m, nh, half] += jnp.dot(
                    a_buf[m, half, xb, yb], b_buf[m, nh, block], preferred_element_type=F32)

    def multiply_near(m, halves, lo, hi):
        @pl.loop(lo, hi)
        def _(step):
            multiply(m, halves, lax.rem(z + 8 + step, 8))

    def multiply_pair(m, halves, step):
        @pl.loop(0, 2)
        def _(way):
            multiply(m, halves, lax.rem(z + 8 + step * (1 - 2 * way), 8))

    reduce = {}

    def r_send(m, nh, lo=0, size=256):
        cols = pl.ds(lo, size)
        reduce[m, nh, lo] = send(part.at[m, nh, 1 - yh, :, cols], landed.at[m, nh, :, cols], to_yh)

    def rotated(m, nh, lo=0, size=256):
        reduce[m, nh, lo].wait_recv()
        cols = pl.ds(lo, size)
        return jnp.transpose(part[m, nh, yh, :, cols] + landed[m, nh, :, cols]).astype(BF16)

    rin = {}

    def i_slices():
        for nh in range(2):
            rin_send[pl.ds(nh * 8, 8)] = rotated(0, nh).reshape(8, 32, 256)
        for d in range(1, 16):
            rin[d] = send(rin_send.at[lax.rem(t + d, 16)], rot_in.at[x, yl, c, t], to_tok[d])
        rot_in[x, yl, c, t] = rin_send[t]

    def i_own():
        for d in range(1, 16):
            rin[d].wait_recv()
        mine = rot_in.at[x, yl, c]
        rin["yl"] = send(mine, mine, to_yl)
        for d in (1, -1):
            rin["own", d] = send(mine, mine, to_x[d])

    def i_other():
        rin["yl"].wait_recv()
        theirs = rot_in.at[x, 1 - yl, c]
        for d in (1, -1):
            rin["other", d] = send(theirs, theirs, to_x[d])

    def i_x2():
        for d in (1, -1):
            rin["own", d].wait_recv()
            rin["other", d].wait_recv()
        for d, lane in ((1, 0), (-1, 1)):
            moved = rot_in.at[xat(-d), lane, c]
            rin["x2", d] = send(moved, moved, to_x[d])

    def i_sib():
        for d in (1, -1):
            rin["x2", d].wait_recv()
        mine = rot_in.at[:, :, c]
        rin["sib"] = send(mine, mine, to_sib)

    gat = {}
    chains = {0: (0, 256, 0), 1: (256, 128, 128)}

    def o_send(key, ref, dev):
        gat[key] = send(ref, ref, dev)

    def o_start(nh):
        lo, size, _ = chains[nh]
        rot_out[t, pl.ds(lo, size)] = rotated(1, nh, 0, size)
        o_single(nh, 1)
        o_cross(nh, 0)

    def o_start_pair(nh):
        lo, single, size = chains[nh]
        rows = pl.ds(lo + single, size)
        rot_out[t, rows] = rotated(1, nh, single, size)
        o_send((nh, "y"), rot_out.at[t, rows], to_yh)

    def o_single(nh, s):
        lo, size, _ = chains[nh]
        for d in (1, -1):
            block = 2 * zat(-(s - 1) * d) + yh
            rows = pl.ds(lo, size) if s < 4 else pl.ds(lo if d == 1 else lo + size // 2, size // 2)
            o_send((nh, "s", s, d), rot_out.at[block, rows], to_z[d])

    def o_cross(nh, s):
        lo, size, _ = chains[nh]
        for d in ((1, -1) if s in (1, 2, 3) else (1,)):
            o_send((nh, "c", s, d), rot_out.at[2 * zat(-s * d) + yh, pl.ds(lo, size)], to_yh)

    def o_pair(nh, s):
        lo, single, size = chains[nh]
        rows = pl.ds(lo + single, size)
        for d in (1, -1):
            block = zat(-(s - 1) * d)
            ref = rot_out.at[pl.ds(2 * block, 2), rows] if s < 4 else rot_out.at[2 * block + (d < 0), rows]
            o_send((nh, "p", s, d), ref, to_z[d])

    def o_wait(nh, kind, s):
        for d in (1, -1):
            if (nh, kind, s, d) in gat:
                gat[nh, kind, s, d].wait_recv()

    def o_pass(nh, s):
        o_wait(nh, "s", s)
        if s < 4:
            o_single(nh, s + 1)
        o_cross(nh, s)

    def o_pass_pair(nh, s):
        if s == 0:
            gat[nh, "y"].wait_recv()
        else:
            o_wait(nh, "p", s)
        o_pair(nh, s + 1)

    def moments(nh, blocks):
        for yb in range(2):
            total = None
            for u in blocks:
                second = labels[u].astype(F32).astype(BF16)
                weights = rot_out[u, pl.ds(nh * 256, 256)]
                mine = rot_in[:, yb, :, u].reshape(256, 256)
                for keep_mask in (second, 1.0 - second):
                    moment = lax.dot_general(mine * keep_mask, weights, (((1,), (1,)), ((), ())),
                                             preferred_element_type=F32)
                    moment = moment * moment
                    total = moment if total is None else total + moment
            out[pl.ds(yb * 256, 256), pl.ds(nh * 256, 256)] += total

    def moments_at(nh, s):
        o_wait(nh, "c", s)
        blocks = []
        for step in ((s,) if s in (0, 4) else (s, -s)):
            block = 2 * zat(step)
            blocks += [block, block + 1]
        moments(nh, blocks)

    n0, n1, both_halves = (0,), (1,), (0, 1)
    a_own(0)
    b_pass(0, 1, True)
    b_pass(0, 1, False)
    a_other(0)
    b_pass(0, 2, True)
    a_x2(0)
    a_own(1)
    b_pass(0, 2, False)
    a_sib(0)
    a_other(1)
    for copy in keep:
        copy.wait()
    b_pass(0, 3, True)
    feat[0, "sib"].wait_recv()
    multiply_near(0, both_halves, -2, 3)
    b_wait(0, 3, False)
    b_send(1, 1, True)
    b_send(1, 1, False)
    multiply_pair(0, both_halves, 3)
    a_x2(1)
    b_wait(0, 4, True)
    multiply(0, both_halves, zat(4))
    r_send(0, 0)
    r_send(0, 1)
    b_pass(1, 1, True)
    a_sib(1)
    b_pass(1, 1, False)
    b_pass(1, 2, True)
    b_pass(1, 2, False)
    feat[1, "sib"].wait_recv()
    b_pass(1, 3, True)
    multiply_near(1, n0, -1, 2)
    b_wait(1, 3, False)
    b_send(2, 1, True)
    b_send(2, 1, False)
    i_slices()
    multiply_pair(1, n0, 2)
    b_wait(1, 4, True)
    multiply_pair(1, n0, 3)
    multiply(1, n0, zat(4))
    r_send(1, 0)
    b_pass(2, 1, True)
    b_pass(2, 1, False)
    i_own()
    b_pass(2, 2, True)
    b_pass(2, 2, False)
    o_start(0)
    multiply_near(1, n1, -1, 2)
    i_other()
    b_pass(2, 3, True)
    o_pass(0, 1)
    b_wait(2, 3, False)
    multiply_pair(1, n1, 2)
    multiply_pair(1, n1, 3)
    i_x2()
    b_wait(2, 4, True)
    multiply(1, n1, zat(4))
    r_send(1, 1, 128, 128)
    r_send(1, 1, 0, 128)
    o_pass(0, 2)
    i_sib()
    o_start_pair(1)
    o_start(1)
    o_pass(0, 3)
    for d in range(1, 16):
        label_copies[d].wait_recv()
    o_pass_pair(1, 0)
    o_pass(0, 4)
    o_pass(1, 1)
    rin["sib"].wait_recv()
    moments_at(0, 0)
    o_pass_pair(1, 1)
    o_pass(1, 2)
    moments_at(0, 1)
    o_pass_pair(1, 2)
    o_pass(1, 3)
    moments_at(0, 2)
    o_pass_pair(1, 3)
    o_pass(1, 4)
    moments_at(0, 3)
    moments_at(0, 4)
    moments_at(1, 0)
    moments_at(1, 1)
    moments_at(1, 2)
    moments_at(1, 3)
    o_wait(1, "p", 4)
    moments_at(1, 4)
    out[...] = out[...] * F32(1.0 / 4096)
    for copy in sent:
        copy.wait_send()


def local(acts, grads, basis_in, basis_out, membership):
    any_space, vmem = pl.BlockSpec(memory_space=pl.ANY), pl.BlockSpec(memory_space=pltpu.VMEM)
    energy = pl.pallas_call(
        kernel,
        out_shape=jax.ShapeDtypeStruct((512, 512), F32),
        in_specs=[any_space] * 4 + [vmem],
        out_specs=vmem,
        scratch_shapes=[
            pltpu.VMEM((2, 2, 4, 2, 256, 512), BF16),
            pltpu.VMEM((2, 2, 8, 512, 256), BF16),
            pltpu.VMEM((2, 2, 2, 256, 256), F32),
            pltpu.VMEM((2, 2, 256, 256), F32),
            pltpu.VMEM((16, 512, 256), BF16),
            pltpu.VMEM((16, 32, 256), BF16),
            pltpu.VMEM((4, 2, 2, 16, 32, 256), BF16),
            pltpu.VMEM((16, 1, 256), jnp.int32),
            pltpu.SemaphoreType.DMA((NSEM,)),
            pltpu.SemaphoreType.DMA((NSEM,)),
            pltpu.SemaphoreType.DMA((6,)),
        ],
        compiler_params=pltpu.CompilerParams(
            collective_id=0, has_side_effects=True, vmem_limit_bytes=56 * 1024 * 1024),
        name="ekfac",
    )(acts, grads, basis_in, basis_out, membership)
    return jnp.transpose(energy.reshape(16, 32, 512), (2, 0, 1))


def solution(mesh):
    placed = (P("tok", "grp"), P("tok", "grp"), P("tok", "grp"), P("tok", "grp"), P("tok", None))
    return jax.shard_map(
        local, mesh=mesh, in_specs=placed, out_specs=P("grp", None, "tok"), check_vma=False
    )
```

```python
import jax
import jax.numpy as jnp
from jax import lax
from jax.experimental import pallas as pl
from jax.experimental.pallas import tpu as pltpu
from jax.sharding import PartitionSpec as P

MESH = pl.DeviceIdType.MESH
F32, BF16 = jnp.float32, jnp.bfloat16
NSEM = 200


def kernel(acts, grads, basis_in, basis_out, membership, out, a_buf, b_buf, part, landed, rot_out,
           rin_send, rot_in, labels, ssem, rsem, lsem):
    g, t = lax.axis_index("grp"), lax.axis_index("tok")
    c, x, yl = lax.rem(g, 2), lax.rem(lax.div(g, 2), 4), lax.div(g, 8)
    z, yh = lax.div(t, 2), lax.rem(t, 2)

    def grp(x_, yl_, c_):
        return (yl_ * 4 + x_) * 2 + c_

    def xat(step):
        return lax.rem(x + 4 + step, 4)

    def zat(step):
        return lax.rem(z + 8 + step, 8)

    to_x = {1: {"grp": grp(xat(1), yl, c)}, -1: {"grp": grp(xat(-1), yl, c)}}
    to_z = {1: {"tok": zat(1) * 2 + yh}, -1: {"tok": zat(-1) * 2 + yh}}
    to_yl = {"grp": grp(x, 1 - yl, c)}
    to_yh = {"tok": z * 2 + 1 - yh}
    to_sib = {"grp": grp(x, yl, 1 - c)}
    to_diag = {"grp": grp(x, yl, 1 - c), "tok": z * 2 + 1 - yh}
    to_tok = [None] + [{"tok": lax.rem(t + d, 16)} for d in range(1, 16)]

    barrier = pltpu.get_barrier_semaphore()
    partners = to_tok[1:] + [to_diag, to_x[1], to_x[-1], to_yl, to_sib]
    for partner in partners:
        pl.semaphore_signal(barrier, inc=1, device_id=partner, device_id_type=MESH)
    pl.semaphore_wait(barrier, len(partners))

    used = [0]
    sent = []

    def make(src, dst, dev):
        at = used[0]
        used[0] += 1
        return pltpu.make_async_remote_copy(
            src_ref=src, dst_ref=dst, send_sem=ssem.at[at], recv_sem=rsem.at[at],
            device_id=dev, device_id_type=MESH)

    def send(src, dst, dev):
        copy = make(src, dst, dev)
        copy.start()
        sent.append(copy)
        return copy

    feats, bases = (acts, grads), (basis_in, basis_out)

    ring = {}

    def b_part(k, block, first, d):
        half = 0 if (d == 1) == first else 1
        if k == 0:
            cols = pl.ds(half * 256, 256)
            return basis_in.at[:, cols], b_buf.at[0, half, block]
        rows, cols = pl.ds(half * 256, 256), pl.ds((k - 1) * 256, 256)
        return basis_out.at[rows, cols], b_buf.at[1, k - 1, block, rows]

    def b_send(k, s, first):
        for d in (1, -1):
            if s == 4 and not first:
                continue
            source, slot = b_part(k, zat(-(s - 1) * d), first, d)
            ring[k, s, first, d] = send(source if s == 1 else slot, slot, to_z[d])

    def b_wait(k, s, first):
        for d in (1, -1):
            ring[k, s, first, d].wait_recv()

    def b_pass(k, s, first):
        b_wait(k, s, first)
        b_send(k, s + 1, first)

    b_send(0, 1, True)
    b_send(0, 1, False)

    diag = [make(feats[m], a_buf.at[m, yh, x, yl], to_diag) for m in range(2)]
    stay = [pltpu.make_async_copy(feats[m], a_buf.at[m, yh, x, yl], lsem.at[m]) for m in range(2)]
    keep = [pltpu.make_async_copy(bases[m].at[:, pl.ds(nh * 256, 256)], b_buf.at[m, nh, z], lsem.at[2 + 2 * m + nh])
            for m in range(2) for nh in range(2)]

    @pl.when(yh != c)
    def _():
        for m in range(2):
            diag[m].start()

    @pl.when(yh == c)
    def _():
        for m in range(2):
            stay[m].start()

    for copy in keep:
        copy.start()
    labels[t] = membership[...]
    mine = labels.at[t]
    label_copies = [None] + [send(mine, mine, to_tok[d]) for d in range(1, 16)]
    part[...] = jnp.zeros_like(part)
    out[...] = jnp.zeros_like(out)

    feat = {}

    def a_diag_wait(m):
        @pl.when(yh != c)
        def _():
            diag[m].wait()

        @pl.when(yh == c)
        def _():
            stay[m].wait()

    def a_own(m):
        a_diag_wait(m)
        mine = a_buf.at[m, c, x, yl]
        feat[m, "yl"] = send(mine, mine, to_yl)
        for d in (1, -1):
            feat[m, "own", d] = send(mine, mine, to_x[d])

    def a_other(m):
        feat[m, "yl"].wait_recv()
        theirs = a_buf.at[m, c, x, 1 - yl]
        for d in (1, -1):
            feat[m, "other", d] = send(theirs, theirs, to_x[d])

    def a_x2(m):
        for d in (1, -1):
            feat[m, "own", d].wait_recv()
            feat[m, "other", d].wait_recv()
        for d, lane in ((1, 0), (-1, 1)):
            moved = a_buf.at[m, c, xat(-d), lane]
            feat[m, "x2", d] = send(moved, moved, to_x[d])

    def a_sib(m):
        for d in (1, -1):
            feat[m, "x2", d].wait_recv()
        mine = a_buf.at[m, c]
        feat[m, "sib"] = send(mine, mine, to_sib)

    def multiply(m, halves, block):
        xb, yb = lax.rem(block, 4), lax.div(block, 4)
        for nh in halves:
            for half in range(2):
                part[m, nh, half] += jnp.dot(
                    a_buf[m, half, xb, yb], b_buf[m, nh, block], preferred_element_type=F32)

    def multiply_near(m, halves, lo, hi):
        @pl.loop(lo, hi)
        def _(step):
            multiply(m, halves, lax.rem(z + 8 + step, 8))

    def multiply_pair(m, halves, step):
        @pl.loop(0, 2)
        def _(way):
            multiply(m, halves, lax.rem(z + 8 + step * (1 - 2 * way), 8))

    reduce = {}

    def r_send(m, nh, lo=0, size=256):
        cols = pl.ds(lo, size)
        reduce[m, nh, lo] = send(part.at[m, nh, 1 - yh, :, cols], landed.at[m, nh, :, cols], to_yh)

    def rotated(m, nh, lo=0, size=256):
        reduce[m, nh, lo].wait_recv()
        cols = pl.ds(lo, size)
        return jnp.transpose(part[m, nh, yh, :, cols] + landed[m, nh, :, cols]).astype(BF16)

    rin = {}

    def i_slices():
        for nh in range(2):
            rin_send[pl.ds(nh * 8, 8)] = rotated(0, nh).reshape(8, 32, 256)
        for d in range(1, 16):
            rin[d] = send(rin_send.at[lax.rem(t + d, 16)], rot_in.at[x, yl, c, t], to_tok[d])
        rot_in[x, yl, c, t] = rin_send[t]

    def i_own():
        for d in range(1, 16):
            rin[d].wait_recv()
        mine = rot_in.at[x, yl, c]
        rin["yl"] = send(mine, mine, to_yl)
        for d in (1, -1):
            rin["own", d] = send(mine, mine, to_x[d])

    def i_other():
        rin["yl"].wait_recv()
        theirs = rot_in.at[x, 1 - yl, c]
        for d in (1, -1):
            rin["other", d] = send(theirs, theirs, to_x[d])

    def i_x2():
        for d in (1, -1):
            rin["own", d].wait_recv()
            rin["other", d].wait_recv()
        for d, lane in ((1, 0), (-1, 1)):
            moved = rot_in.at[xat(-d), lane, c]
            rin["x2", d] = send(moved, moved, to_x[d])

    def i_sib():
        for d in (1, -1):
            rin["x2", d].wait_recv()
        mine = rot_in.at[:, :, c]
        rin["sib"] = send(mine, mine, to_sib)

    gat = {}
    chains = {0: (0, 192, 64), 1: (256, 128, 128)}

    def o_send(key, ref, dev):
        gat[key] = send(ref, ref, dev)

    def o_start(nh):
        lo, size, _ = chains[nh]
        rot_out[t, pl.ds(lo, size)] = rotated(1, nh, 0, size)
        o_single(nh, 1)
        o_cross(nh, 0)

    def o_start_pair(nh):
        lo, single, size = chains[nh]
        rows = pl.ds(lo + single, size)
        rot_out[t, rows] = rotated(1, nh, single, size)
        o_send((nh, "y"), rot_out.at[t, rows], to_yh)

    def o_begin(nh):
        lo, single, size = chains[nh]
        rot_out[t, pl.ds(nh * 256, 256)] = rotated(1, nh)
        o_single(nh, 1)
        o_send((nh, "y"), rot_out.at[t, pl.ds(lo + single, size)], to_yh)
        o_cross(nh, 0)

    def o_single(nh, s):
        lo, size, _ = chains[nh]
        for d in (1, -1):
            block = 2 * zat(-(s - 1) * d) + yh
            rows = pl.ds(lo, size) if s < 4 else pl.ds(lo if d == 1 else lo + size // 2, size // 2)
            o_send((nh, "s", s, d), rot_out.at[block, rows], to_z[d])

    def o_cross(nh, s):
        lo, size, _ = chains[nh]
        for d in ((1, -1) if s in (1, 2, 3) else (1,)):
            o_send((nh, "c", s, d), rot_out.at[2 * zat(-s * d) + yh, pl.ds(lo, size)], to_yh)

    def o_pair(nh, s):
        lo, single, size = chains[nh]
        rows = pl.ds(lo + single, size)
        for d in (1, -1):
            block = zat(-(s - 1) * d)
            ref = rot_out.at[pl.ds(2 * block, 2), rows] if s < 4 else rot_out.at[2 * block + (d < 0), rows]
            o_send((nh, "p", s, d), ref, to_z[d])

    def o_wait(nh, kind, s):
        for d in (1, -1):
            if (nh, kind, s, d) in gat:
                gat[nh, kind, s, d].wait_recv()

    def o_pass(nh, s):
        o_wait(nh, "s", s)
        o_cross(nh, s)
        if s < 4:
            o_single(nh, s + 1)

    def o_pass_pair(nh, s):
        if s == 0:
            gat[nh, "y"].wait_recv()
        else:
            o_wait(nh, "p", s)
        o_pair(nh, s + 1)

    def moments(nh, blocks):
        for yb in range(2):
            total = None
            for u in blocks:
                second = labels[u].astype(F32).astype(BF16)
                weights = rot_out[u, pl.ds(nh * 256, 256)]
                mine = rot_in[:, yb, :, u].reshape(256, 256)
                for keep_mask in (second, 1.0 - second):
                    moment = lax.dot_general(mine * keep_mask, weights, (((1,), (1,)), ((), ())),
                                             preferred_element_type=F32)
                    moment = moment * moment
                    total = moment if total is None else total + moment
            out[pl.ds(yb * 256, 256), pl.ds(nh * 256, 256)] += total

    def moments_at(nh, s):
        o_wait(nh, "c", s)
        blocks = []
        for step in ((s,) if s in (0, 4) else (s, -s)):
            block = 2 * zat(step)
            blocks += [block, block + 1]
        moments(nh, blocks)

    n0, n1, both_halves = (0,), (1,), (0, 1)
    a_own(0)
    b_pass(0, 1, True)
    b_pass(0, 1, False)
    a_other(0)
    b_pass(0, 2, True)
    a_x2(0)
    a_own(1)
    b_pass(0, 2, False)
    a_sib(0)
    a_other(1)
    for copy in keep:
        copy.wait()
    b_pass(0, 3, True)
    feat[0, "sib"].wait_recv()
    multiply_near(0, both_halves, -2, 3)
    b_wait(0, 3, False)
    b_send(1, 1, True)
    b_send(1, 1, False)
    multiply_pair(0, both_halves, 3)
    a_x2(1)
    b_wait(0, 4, True)
    multiply(0, both_halves, zat(4))
    r_send(0, 0)
    r_send(0, 1)
    b_pass(1, 1, True)
    a_sib(1)
    b_pass(1, 1, False)
    b_pass(1, 2, True)
    b_pass(1, 2, False)
    feat[1, "sib"].wait_recv()
    b_pass(1, 3, True)
    multiply_near(1, n0, -1, 2)
    b_wait(1, 3, False)
    b_send(2, 1, True)
    b_send(2, 1, False)
    i_slices()
    multiply_pair(1, n0, 2)
    b_wait(1, 4, True)
    multiply_pair(1, n0, 3)
    multiply(1, n0, zat(4))
    r_send(1, 0)
    b_pass(2, 1, True)
    b_pass(2, 1, False)
    i_own()
    b_pass(2, 2, True)
    b_pass(2, 2, False)
    o_begin(0)
    multiply_near(1, n1, -1, 2)
    i_other()
    o_pass_pair(0, 0)
    b_pass(2, 3, True)
    o_pass(0, 1)
    b_wait(2, 3, False)
    multiply_pair(1, n1, 2)
    multiply_pair(1, n1, 3)
    i_x2()
    b_wait(2, 4, True)
    multiply(1, n1, zat(4))
    r_send(1, 1, 128, 128)
    r_send(1, 1, 0, 128)
    o_pass(0, 2)
    o_pass_pair(0, 1)
    i_sib()
    o_start_pair(1)
    o_start(1)
    o_pass(0, 3)
    o_pass_pair(0, 2)
    for d in range(1, 16):
        label_copies[d].wait_recv()
    o_pass_pair(1, 0)
    o_pass(0, 4)
    o_pass_pair(0, 3)
    o_pass(1, 1)
    rin["sib"].wait_recv()
    moments_at(0, 0)
    o_pass_pair(1, 1)
    o_pass(1, 2)
    moments_at(0, 1)
    o_pass_pair(1, 2)
    o_pass(1, 3)
    moments_at(0, 2)
    o_pass_pair(1, 3)
    o_pass(1, 4)
    moments_at(0, 3)
    o_wait(0, "p", 4)
    moments_at(0, 4)
    moments_at(1, 0)
    moments_at(1, 1)
    moments_at(1, 2)
    moments_at(1, 3)
    o_wait(1, "p", 4)
    moments_at(1, 4)
    for copy in sent:
        copy.wait_send()


def local(acts, grads, basis_in, basis_out, membership):
    any_space, vmem = pl.BlockSpec(memory_space=pl.ANY), pl.BlockSpec(memory_space=pltpu.VMEM)
    energy = pl.pallas_call(
        kernel,
        out_shape=jax.ShapeDtypeStruct((512, 512), F32),
        in_specs=[any_space] * 4 + [vmem],
        out_specs=vmem,
        scratch_shapes=[
            pltpu.VMEM((2, 2, 4, 2, 256, 512), BF16),
            pltpu.VMEM((2, 2, 8, 512, 256), BF16),
            pltpu.VMEM((2, 2, 2, 256, 256), F32),
            pltpu.VMEM((2, 2, 256, 256), F32),
            pltpu.VMEM((16, 512, 256), BF16),
            pltpu.VMEM((16, 32, 256), BF16),
            pltpu.VMEM((4, 2, 2, 16, 32, 256), BF16),
            pltpu.VMEM((16, 1, 256), jnp.int32),
            pltpu.SemaphoreType.DMA((NSEM,)),
            pltpu.SemaphoreType.DMA((NSEM,)),
            pltpu.SemaphoreType.DMA((6,)),
        ],
        compiler_params=pltpu.CompilerParams(
            collective_id=0, has_side_effects=True, vmem_limit_bytes=56 * 1024 * 1024),
        name="ekfac",
    )(acts, grads, basis_in, basis_out, membership)
    return jnp.transpose(energy.reshape(16, 32, 512), (2, 0, 1)) * F32(1.0 / 4096)


def solution(mesh):
    placed = (P("tok", "grp"), P("tok", "grp"), P("tok", "grp"), P("tok", "grp"), P("tok", None))
    return jax.shard_map(
        local, mesh=mesh, in_specs=placed, out_specs=P("grp", None, "tok"), check_vma=False
    )
```

```python
import jax
import jax.numpy as jnp
from jax import lax
from jax.experimental import pallas as pl
from jax.experimental.pallas import tpu as pltpu
from jax.sharding import PartitionSpec as P

MESH = pl.DeviceIdType.MESH
F32, BF16 = jnp.float32, jnp.bfloat16
NSEM = 200


def kernel(acts, grads, basis_in, basis_out, membership, out, a_buf, b_buf, part, landed, rot_out,
           rin_send, rot_in, labels, ssem, rsem, lsem):
    g, t = lax.axis_index("grp"), lax.axis_index("tok")
    c, x, yl = lax.rem(g, 2), lax.rem(lax.div(g, 2), 4), lax.div(g, 8)
    z, yh = lax.div(t, 2), lax.rem(t, 2)

    def grp(x_, yl_, c_):
        return (yl_ * 4 + x_) * 2 + c_

    def xat(step):
        return lax.rem(x + 4 + step, 4)

    def zat(step):
        return lax.rem(z + 8 + step, 8)

    to_x = {1: {"grp": grp(xat(1), yl, c)}, -1: {"grp": grp(xat(-1), yl, c)}}
    to_z = {1: {"tok": zat(1) * 2 + yh}, -1: {"tok": zat(-1) * 2 + yh}}
    to_yl = {"grp": grp(x, 1 - yl, c)}
    to_yh = {"tok": z * 2 + 1 - yh}
    to_sib = {"grp": grp(x, yl, 1 - c)}
    to_diag = {"grp": grp(x, yl, 1 - c), "tok": z * 2 + 1 - yh}
    to_tok = [None] + [{"tok": lax.rem(t + d, 16)} for d in range(1, 16)]

    barrier = pltpu.get_barrier_semaphore()
    partners = to_tok[1:] + [to_diag, to_x[1], to_x[-1], to_yl, to_sib]
    for partner in partners:
        pl.semaphore_signal(barrier, inc=1, device_id=partner, device_id_type=MESH)
    pl.semaphore_wait(barrier, len(partners))

    used = [0]
    sent = []

    def make(src, dst, dev):
        at = used[0]
        used[0] += 1
        return pltpu.make_async_remote_copy(
            src_ref=src, dst_ref=dst, send_sem=ssem.at[at], recv_sem=rsem.at[at],
            device_id=dev, device_id_type=MESH)

    def send(src, dst, dev):
        copy = make(src, dst, dev)
        copy.start()
        sent.append(copy)
        return copy

    feats, bases = (acts, grads), (basis_in, basis_out)

    ring = {}

    def b_part(k, block, first, d):
        half = 0 if (d == 1) == first else 1
        if k == 0:
            cols = pl.ds(half * 256, 256)
            return basis_in.at[:, cols], b_buf.at[0, half, block]
        rows, cols = pl.ds(half * 256, 256), pl.ds((k - 1) * 256, 256)
        return basis_out.at[rows, cols], b_buf.at[1, k - 1, block, rows]

    def b_send(k, s, first):
        for d in (1, -1):
            if s == 4 and not first:
                continue
            source, slot = b_part(k, zat(-(s - 1) * d), first, d)
            ring[k, s, first, d] = send(source if s == 1 else slot, slot, to_z[d])

    def b_wait(k, s, first):
        for d in (1, -1):
            ring[k, s, first, d].wait_recv()

    def b_pass(k, s, first):
        b_wait(k, s, first)
        b_send(k, s + 1, first)

    b_send(0, 1, True)
    b_send(0, 1, False)

    diag = [make(feats[m], a_buf.at[m, yh, x, yl], to_diag) for m in range(2)]
    stay = [pltpu.make_async_copy(feats[m], a_buf.at[m, yh, x, yl], lsem.at[m]) for m in range(2)]
    keep = [pltpu.make_async_copy(bases[m].at[:, pl.ds(nh * 256, 256)], b_buf.at[m, nh, z], lsem.at[2 + 2 * m + nh])
            for m in range(2) for nh in range(2)]

    @pl.when(yh != c)
    def _():
        for m in range(2):
            diag[m].start()

    @pl.when(yh == c)
    def _():
        for m in range(2):
            stay[m].start()

    for copy in keep:
        copy.start()
    labels[t] = membership[...]
    mine = labels.at[t]
    label_copies = [None] + [send(mine, mine, to_tok[d]) for d in range(1, 16)]
    part[...] = jnp.zeros_like(part)
    out[...] = jnp.zeros_like(out)

    feat = {}

    def a_diag_wait(m):
        @pl.when(yh != c)
        def _():
            diag[m].wait()

        @pl.when(yh == c)
        def _():
            stay[m].wait()

    def a_own(m):
        a_diag_wait(m)
        mine = a_buf.at[m, c, x, yl]
        feat[m, "yl"] = send(mine, mine, to_yl)
        for d in (1, -1):
            feat[m, "own", d] = send(mine, mine, to_x[d])

    def a_other(m):
        feat[m, "yl"].wait_recv()
        theirs = a_buf.at[m, c, x, 1 - yl]
        for d in (1, -1):
            feat[m, "other", d] = send(theirs, theirs, to_x[d])

    def a_x2(m):
        for d in (1, -1):
            feat[m, "own", d].wait_recv()
            feat[m, "other", d].wait_recv()
        for d, lane in ((1, 0), (-1, 1)):
            moved = a_buf.at[m, c, xat(-d), lane]
            feat[m, "x2", d] = send(moved, moved, to_x[d])

    def a_sib(m):
        for d in (1, -1):
            feat[m, "x2", d].wait_recv()
        mine = a_buf.at[m, c]
        feat[m, "sib"] = send(mine, mine, to_sib)

    def multiply(m, halves, block):
        xb, yb = lax.rem(block, 4), lax.div(block, 4)
        for nh in halves:
            for half in range(2):
                part[m, nh, half] += jnp.dot(
                    a_buf[m, half, xb, yb], b_buf[m, nh, block], preferred_element_type=F32)

    def multiply_near(m, halves, lo, hi):
        @pl.loop(lo, hi)
        def _(step):
            multiply(m, halves, lax.rem(z + 8 + step, 8))

    def multiply_pair(m, halves, step):
        @pl.loop(0, 2)
        def _(way):
            multiply(m, halves, lax.rem(z + 8 + step * (1 - 2 * way), 8))

    reduce = {}

    def r_send(m, nh, lo=0, size=256):
        cols = pl.ds(lo, size)
        reduce[m, nh, lo] = send(part.at[m, nh, 1 - yh, :, cols], landed.at[m, nh, :, cols], to_yh)

    def rotated(m, nh, lo=0, size=256):
        reduce[m, nh, lo].wait_recv()
        cols = pl.ds(lo, size)
        return jnp.transpose(part[m, nh, yh, :, cols] + landed[m, nh, :, cols]).astype(BF16)

    rin = {}

    def i_slices():
        for nh in range(2):
            rin_send[pl.ds(nh * 8, 8)] = rotated(0, nh).reshape(8, 32, 256)
        for d in range(1, 16):
            rin[d] = send(rin_send.at[lax.rem(t + d, 16)], rot_in.at[x, yl, c, t], to_tok[d])
        rot_in[x, yl, c, t] = rin_send[t]

    def i_own():
        for d in range(1, 16):
            rin[d].wait_recv()
        mine = rot_in.at[x, yl, c]
        rin["yl"] = send(mine, mine, to_yl)
        for d in (1, -1):
            rin["own", d] = send(mine, mine, to_x[d])

    def i_other():
        rin["yl"].wait_recv()
        theirs = rot_in.at[x, 1 - yl, c]
        for d in (1, -1):
            rin["other", d] = send(theirs, theirs, to_x[d])

    def i_x2():
        for d in (1, -1):
            rin["own", d].wait_recv()
            rin["other", d].wait_recv()
        for d, lane in ((1, 0), (-1, 1)):
            moved = rot_in.at[xat(-d), lane, c]
            rin["x2", d] = send(moved, moved, to_x[d])

    def i_sib():
        for d in (1, -1):
            rin["x2", d].wait_recv()
        mine = rot_in.at[:, :, c]
        rin["sib"] = send(mine, mine, to_sib)

    gat = {}
    chains = {0: (0, 192, 64), 1: (256, 128, 128)}

    def o_send(key, ref, dev):
        gat[key] = send(ref, ref, dev)

    def o_start(nh):
        lo, size, _ = chains[nh]
        rot_out[t, pl.ds(lo, size)] = rotated(1, nh, 0, size)
        o_single(nh, 1)
        o_cross(nh, 0)

    def o_start_pair(nh):
        lo, single, size = chains[nh]
        rows = pl.ds(lo + single, size)
        rot_out[t, rows] = rotated(1, nh, single, size)
        o_send((nh, "y"), rot_out.at[t, rows], to_yh)

    def o_begin(nh):
        lo, single, size = chains[nh]
        rot_out[t, pl.ds(nh * 256, 256)] = rotated(1, nh)
        o_single(nh, 1)
        o_send((nh, "y"), rot_out.at[t, pl.ds(lo + single, size)], to_yh)
        o_cross(nh, 0)

    def o_single(nh, s):
        lo, size, _ = chains[nh]
        for d in (1, -1):
            block = 2 * zat(-(s - 1) * d) + yh
            rows = pl.ds(lo, size) if s < 4 else pl.ds(lo if d == 1 else lo + size // 2, size // 2)
            o_send((nh, "s", s, d), rot_out.at[block, rows], to_z[d])

    def o_cross(nh, s):
        lo, size, _ = chains[nh]
        for d in ((1, -1) if s in (1, 2, 3) else (1,)):
            o_send((nh, "c", s, d), rot_out.at[2 * zat(-s * d) + yh, pl.ds(lo, size)], to_yh)

    def o_pair(nh, s):
        lo, single, size = chains[nh]
        rows = pl.ds(lo + single, size)
        for d in (1, -1):
            block = zat(-(s - 1) * d)
            ref = rot_out.at[pl.ds(2 * block, 2), rows] if s < 4 else rot_out.at[2 * block + (d < 0), rows]
            o_send((nh, "p", s, d), ref, to_z[d])

    def o_wait(nh, kind, s):
        for d in (1, -1):
            if (nh, kind, s, d) in gat:
                gat[nh, kind, s, d].wait_recv()

    def o_pass(nh, s):
        if s == 4:
            lo, size, _ = chains[nh]
            for d in (1, -1):
                gat[nh, "s", 4, d].wait_recv()
                rows = pl.ds(lo if d == 1 else lo + size // 2, size // 2)
                o_send((nh, "c", 4, d), rot_out.at[2 * zat(4) + yh, rows], to_yh)
            return
        o_wait(nh, "s", s)
        o_cross(nh, s)
        if s < 4:
            o_single(nh, s + 1)

    def o_pass_pair(nh, s):
        if s == 0:
            gat[nh, "y"].wait_recv()
        else:
            o_wait(nh, "p", s)
        o_pair(nh, s + 1)

    def moments(nh, blocks):
        for yb in range(2):
            total = None
            for u in blocks:
                second = labels[u].astype(F32).astype(BF16)
                weights = rot_out[u, pl.ds(nh * 256, 256)]
                mine = rot_in[:, yb, :, u].reshape(256, 256)
                for keep_mask in (second, 1.0 - second):
                    moment = lax.dot_general(mine * keep_mask, weights, (((1,), (1,)), ((), ())),
                                             preferred_element_type=F32)
                    moment = moment * moment
                    total = moment if total is None else total + moment
            out[pl.ds(yb * 256, 256), pl.ds(nh * 256, 256)] += total

    def moments_at(nh, s):
        o_wait(nh, "c", s)
        blocks = []
        for step in ((s,) if s in (0, 4) else (s, -s)):
            block = 2 * zat(step)
            blocks += [block, block + 1]
        moments(nh, blocks)

    n0, n1, both_halves = (0,), (1,), (0, 1)
    a_own(0)
    b_pass(0, 1, True)
    b_pass(0, 1, False)
    a_other(0)
    b_pass(0, 2, True)
    a_x2(0)
    a_own(1)
    b_pass(0, 2, False)
    a_sib(0)
    a_other(1)
    for copy in keep:
        copy.wait()
    b_pass(0, 3, True)
    feat[0, "sib"].wait_recv()
    multiply_near(0, both_halves, -2, 3)
    b_wait(0, 3, False)
    b_send(1, 1, True)
    b_send(1, 1, False)
    multiply_pair(0, both_halves, 3)
    a_x2(1)
    b_wait(0, 4, True)
    multiply(0, both_halves, zat(4))
    r_send(0, 0)
    r_send(0, 1)
    b_pass(1, 1, True)
    a_sib(1)
    b_pass(1, 1, False)
    b_pass(1, 2, True)
    b_pass(1, 2, False)
    feat[1, "sib"].wait_recv()
    b_pass(1, 3, True)
    multiply_near(1, n0, -1, 2)
    b_wait(1, 3, False)
    b_send(2, 1, True)
    b_send(2, 1, False)
    i_slices()
    multiply_pair(1, n0, 2)
    b_wait(1, 4, True)
    multiply_pair(1, n0, 3)
    multiply(1, n0, zat(4))
    r_send(1, 0)
    b_pass(2, 1, True)
    b_pass(2, 1, False)
    i_own()
    b_pass(2, 2, True)
    b_pass(2, 2, False)
    o_begin(0)
    multiply_near(1, n1, -1, 2)
    i_other()
    o_pass_pair(0, 0)
    b_pass(2, 3, True)
    o_pass(0, 1)
    b_wait(2, 3, False)
    multiply_pair(1, n1, 2)
    multiply_pair(1, n1, 3)
    i_x2()
    b_wait(2, 4, True)
    multiply(1, n1, zat(4))
    r_send(1, 1, 128, 128)
    r_send(1, 1, 0, 128)
    o_pass(0, 2)
    o_pass_pair(0, 1)
    i_sib()
    o_start_pair(1)
    o_start(1)
    o_pass(0, 3)
    o_pass_pair(0, 2)
    for d in range(1, 16):
        label_copies[d].wait_recv()
    o_pass_pair(1, 0)
    o_pass(0, 4)
    o_pass_pair(0, 3)
    o_pass(1, 1)
    rin["sib"].wait_recv()
    moments_at(0, 0)
    o_pass_pair(1, 1)
    o_pass(1, 2)
    moments_at(0, 1)
    o_pass_pair(1, 2)
    o_pass(1, 3)
    moments_at(0, 2)
    o_pass_pair(1, 3)
    o_pass(1, 4)
    moments_at(0, 3)
    o_wait(0, "p", 4)
    moments_at(0, 4)
    moments_at(1, 0)
    moments_at(1, 1)
    moments_at(1, 2)
    moments_at(1, 3)
    o_wait(1, "p", 4)
    moments_at(1, 4)
    for copy in sent:
        copy.wait_send()


def local(acts, grads, basis_in, basis_out, membership):
    any_space, vmem = pl.BlockSpec(memory_space=pl.ANY), pl.BlockSpec(memory_space=pltpu.VMEM)
    energy = pl.pallas_call(
        kernel,
        out_shape=jax.ShapeDtypeStruct((512, 512), F32),
        in_specs=[any_space] * 4 + [vmem],
        out_specs=vmem,
        scratch_shapes=[
            pltpu.VMEM((2, 2, 4, 2, 256, 512), BF16),
            pltpu.VMEM((2, 2, 8, 512, 256), BF16),
            pltpu.VMEM((2, 2, 2, 256, 256), F32),
            pltpu.VMEM((2, 2, 256, 256), F32),
            pltpu.VMEM((16, 512, 256), BF16),
            pltpu.VMEM((16, 32, 256), BF16),
            pltpu.VMEM((4, 2, 2, 16, 32, 256), BF16),
            pltpu.VMEM((16, 1, 256), jnp.int32),
            pltpu.SemaphoreType.DMA((NSEM,)),
            pltpu.SemaphoreType.DMA((NSEM,)),
            pltpu.SemaphoreType.DMA((6,)),
        ],
        compiler_params=pltpu.CompilerParams(
            collective_id=0, has_side_effects=True, vmem_limit_bytes=56 * 1024 * 1024),
        name="ekfac",
    )(acts, grads, basis_in, basis_out, membership)
    return jnp.transpose(energy.reshape(16, 32, 512), (2, 0, 1)) * F32(1.0 / 4096)


def solution(mesh):
    placed = (P("tok", "grp"), P("tok", "grp"), P("tok", "grp"), P("tok", "grp"), P("tok", None))
    return jax.shard_map(
        local, mesh=mesh, in_specs=placed, out_specs=P("grp", None, "tok"), check_vma=False
    )
```
